1024 devices in a mesh: row: 16 (over x, y_lo), col: 32 (over z, core), layer: 2 (over y_hi).
Axes of the slice: x: 4, y: 8 (y_hi: 2, y_lo: 4; y = y_hi * 4 + y_lo), z: 16, core: 2. Of those that a mesh axis runs over, the one named last changes fastest.
Arguments:
- tile_data: bfloat16 [16, 32, 3, 128, 128], P('row', 'col'), may hold values from -0.5 to 0.5
- block_rows: int32 [16, 32, 3], P('row', 'col'), may hold values from 0 to 3, as said below
- block_cols: int32 [16, 32, 3], P('row', 'col'), may hold values from 0 to 1
- filled_count: int32 [16, 32], P('row', 'col'), may hold values from 1 to 3, as said below
Outputs:
- product: float32 [8192, 8192], P(('row', 'layer'), 'col')
The draws below stay inside these ranges and needn't reach their ends.
Inputs may be any that keep to these rules, and one draw needn't show every extreme that they name: `block_rows`: within one grid cell the first filled_count slots name distinct block positions. `filled_count`: some grid cell has all 3 slots filled.
All inputs are finite; a program needn't handle non-finite values.
Results may differ from the reference program's by a relative error of at most 0.0003.
Values may be sent and summed in bfloat16 or wider, within the bound.
A program may use at most 64 MiB of HBM per device.

```python
import jax
import jax.numpy as jnp
from jax import lax

TILE = 128
BC = 2
S = 3
BR = 4
NB = 64
N_ROW = 16
N_COL = 32


def tile_layout(key):
    cells = N_ROW * N_COL
    positions = BR * BC
    key_one, key_two, key_full, key_place = jax.random.split(key, 4)
    count_one = jax.random.randint(key_one, (cells,), 1, S + 1)
    count_two = jax.random.randint(key_two, (cells,), 1, S + 1)
    counts = jnp.minimum(count_one, count_two)
    fullest = jax.random.randint(key_full, (), 0, cells)
    counts = jnp.where(jnp.arange(cells) == fullest, S, counts)
    scores = jax.random.randint(key_place, (cells, positions), 0, 1 << 20) * positions + jnp.arange(positions)[None, :]
    chosen = jnp.argsort(scores, axis=1)[:, :S]
    counts = counts.reshape(N_ROW, N_COL).astype(jnp.int32)
    row_index = (chosen // BC).reshape(N_ROW, N_COL, S).astype(jnp.int32)
    col_index = (chosen % BC).reshape(N_ROW, N_COL, S).astype(jnp.int32)
    return (counts, row_index, col_index)


def draw_filled_count(key, part):
    layout = tile_layout(key)
    return layout[0]


def draw_block_rows(key, part):
    layout = tile_layout(key)
    return layout[1]


def draw_block_cols(key, part):
    layout = tile_layout(key)
    return layout[2]


def block_scale(key, dims, shards, least, largest):
    def one(dim, blocks):
        draws = jax.random.uniform(jax.random.fold_in(jax.random.fold_in(key, 6), dim), (blocks,), jnp.float32, least / len(shards), largest / len(shards))
        return jnp.repeat(jnp.exp(draws), dims[dim] // blocks).reshape((-1,) + (1,) * (len(dims) - dim - 1))

    gain = one(*shards[0])
    for cut in shards[1:]:
        gain = gain * one(*cut)
    return gain


def normal_values(own_key, dims, width, bound, cuts=(), dtype=jnp.bfloat16):
    loudness = block_scale(own_key, dims, cuts, -0.22, 0.18) if cuts else 1.0
    result = jax.random.normal(own_key, dims, jnp.float32) * width * loudness
    return jnp.minimum(jnp.maximum(result, -bound), bound).astype(dtype)


def setup_inputs(seed: int = 0) -> dict:
    arg_keys = jax.random.split(jax.random.key(seed), 5)
    return {
        "tile_data": normal_values(arg_keys[0], (N_ROW, N_COL, S, TILE, TILE), TILE ** -0.5, 0.5, ((0, 16), (1, 32))),
        "block_rows": draw_block_rows(jax.random.fold_in(arg_keys[4], 71), 0),
        "block_cols": draw_block_cols(jax.random.fold_in(arg_keys[4], 71), 0),
        "filled_count": draw_filled_count(jax.random.fold_in(arg_keys[4], 71), 0),
    }


def reference(tile_data, block_rows, block_cols, filled_count):
    grid_rows, grid_cols, slot_count = block_rows.shape
    tile_width = tile_data.shape[-1]
    flat_tiles = tile_data.reshape(grid_rows * grid_cols * slot_count, tile_width, tile_width)
    rows_flat = block_rows.reshape(-1).astype(jnp.int32)
    cols_flat = block_cols.reshape(-1).astype(jnp.int32)
    live_flat = (jnp.arange(slot_count)[None, None, :] < filled_count[:, :, None]).reshape(-1)

    def over_left(position, product):
        position = jnp.asarray(position).astype(jnp.int32)
        cell_row = position // (grid_cols * slot_count)
        cell_col = (position // slot_count) % grid_cols
        row_block = cell_row * BR + rows_flat[position]
        inner_block = cell_col * BC + cols_flat[position]
        source_row = inner_block // BR
        within_row = inner_block % BR
        left_tile = flat_tiles[position]
        left_live = live_flat[position]

        def over_right(partner, carried):
            partner = jnp.asarray(partner).astype(jnp.int32)
            partner_col = partner // slot_count
            target = (source_row * grid_cols + partner_col) * slot_count + partner % slot_count
            matched = left_live & live_flat[target] & (rows_flat[target] == within_row)
            tile_term = lax.cond(
                matched,
                lambda: jnp.dot(left_tile, flat_tiles[target], preferred_element_type=jnp.float32),
                lambda: jnp.zeros((tile_width, tile_width), jnp.float32),
            )
            column_block = partner_col * BC + cols_flat[target]
            start_row = (row_block * tile_width).astype(jnp.int32)
            start_col = (column_block * tile_width).astype(jnp.int32)
            before = lax.dynamic_slice(carried, (start_row, start_col), (tile_width, tile_width))
            return lax.dynamic_update_slice(carried, before + tile_term, (start_row, start_col))

        return lax.fori_loop(0, grid_cols * slot_count, over_right, product)

    product = jnp.zeros((NB * tile_width, NB * tile_width), jnp.float32)
    return lax.fori_loop(0, grid_rows * grid_cols * slot_count, over_left, product)
```

```python
import functools

import jax
import jax.numpy as jnp
from jax import lax
from jax.experimental import pallas as pl
from jax.experimental.pallas import tpu as pltpu
from jax.sharding import PartitionSpec as P

TILE = 128
SLOTS = 3
NX, NY, NZ = 4, 8, 16
Y_LO = 4
N_ROW = 16
N_COL = 32
MARK = 16
ROWS = SLOTS * TILE + MARK
CHUNKS = ((0, 128), (128, 128), (256, 144))
FIRST, SECOND = (0, 208), (208, 192)
MESH = pl.DeviceIdType.MESH


def kernel(
    rows_ref, cols_ref, count_ref, tiles_ref, out_ref,
    left, right, own_sem,
    ring_s, ring_r, far_s, far_r, twin_s, twin_r, grid_s, grid_r,
):
    row = lax.axis_index("row")
    col = lax.axis_index("col")
    layer = lax.axis_index("layer")
    x, y = row // Y_LO, layer * Y_LO + row % Y_LO
    z, core = col // 2, col % 2
    fx, fy, gx, gy = 1 - core, core, core, 1 - core
    away = 1 - 2 * core

    def at_xy(dx, dy):
        nx, ny = (x + dx + NX) % NX, (y + dy + NY) % NY
        return (nx * Y_LO + ny % Y_LO, col, ny // Y_LO)

    def at_z(dz):
        return (row, ((z + dz + NZ) % NZ) * 2 + core, layer)

    twin = (row, z * 2 + 1 - core, layer)

    def left_slot(dz, own):
        return ((z + dz + NZ) % NZ) * 2 + (core if own else 1 - core)

    def right_slot(f, g):
        cx = (x + f * fx + g * gx + NX) % NX
        cy = (y + f * fy + g * gy + NY) % Y_LO
        return cx * Y_LO + cy

    def remote(ref, slot, span, send, recv, device):
        part = ref.at[slot, pl.ds(span[0], span[1])]
        return pltpu.make_async_remote_copy(
            src_ref=part, dst_ref=part, send_sem=send, recv_sem=recv,
            device_id=device, device_id_type=MESH,
        )

    whole = (0, ROWS)

    def ring(way, dist, k):
        w = 0 if way > 0 else 1
        return remote(
            left, left_slot(-way * dist, True), CHUNKS[k],
            ring_s.at[w, dist, k], ring_r.at[w, dist, k], at_z(way),
        )

    def ring_in(way, dist, k):
        w = 0 if way > 0 else 1
        return remote(
            left, left_slot(-way * dist, True), CHUNKS[k],
            ring_s.at[w, dist - 1, k], ring_r.at[w, dist - 1, k], at_z(way),
        )

    def far(k):
        return remote(left, left_slot(-7 * away, True), CHUNKS[k], far_s.at[k], far_r.at[k], at_z(away))

    def far_in(k):
        return remote(left, left_slot(8, True), CHUNKS[k], far_s.at[k], far_r.at[k], at_z(away))

    def to_twin(dz, m, k):
        return remote(left, left_slot(dz, True), CHUNKS[k], twin_s.at[m, k], twin_r.at[m, k], twin)

    def from_twin(dz, m, k):
        return remote(left, left_slot(dz, False), CHUNKS[k], twin_s.at[m, k], twin_r.at[m, k], twin)

    def along(n, f, g, span, first, way):
        step = way if first else 0
        dev = at_xy(way * fx, way * fy) if first else at_xy(way * gx, way * gy)
        return remote(right, right_slot(f, g), span, grid_s.at[n], grid_r.at[n], dev)

    moves = {}
    moves[0] = (0, 0, whole, True, 1)
    moves[1] = (0, 0, whole, True, -1)
    moves[2] = (-1, 0, FIRST, True, 1)
    moves[3] = (1, 0, SECOND, True, -1)
    for i, f in enumerate((0, -1, 1, 2)):
        moves[4 + 4 * i] = (f, 0, whole, False, 1)
        moves[5 + 4 * i] = (f, 0, whole, False, -1)
        moves[6 + 4 * i] = (f, -1, FIRST, False, 1)
        moves[7 + 4 * i] = (f, 1, SECOND, False, -1)

    def go(n):
        along(n, *moves[n]).start()

    def come(n):
        f, g, span, first, way = moves[n]
        if first:
            along(n, f - way, g, span, first, way).wait_recv()
        else:
            along(n, f, g - way, span, first, way).wait_recv()

    def add(m, q):
        half = (m + 1) // 2
        dz = jnp.where(m % 2 == 0, half, -half)
        r = (z + dz + NZ) % NZ
        lslot = r * 2 + q

        def picked(ref, slot, codes):
            marks = ref[slot, pl.ds(SLOTS * TILE, MARK), :].astype(jnp.float32)
            tiles = [ref[slot, pl.ds(s * TILE, TILE), :] for s in range(SLOTS)]
            result = []
            for code in codes:
                total = None
                for s in range(SLOTS):
                    hit = jnp.where(marks[s:s + 1, :] == code, 1.0, 0.0).astype(jnp.bfloat16)
                    term = tiles[s] * hit
                    total = term if total is None else total + term
                result.append(total)
            return result

        base = (4 * layer).astype(jnp.float32)
        a = picked(left, lslot, [base + i for i in range(4)])
        b = picked(right, r, [float(4 * q + i) for i in range(4)])
        lhs = jnp.concatenate([jnp.concatenate(a[:2], axis=1), jnp.concatenate(a[2:], axis=1)], axis=0)
        rhs = jnp.concatenate([jnp.concatenate(b[:2], axis=1), jnp.concatenate(b[2:], axis=1)], axis=0)
        out_ref[...] += jnp.dot(lhs, rhs, preferred_element_type=jnp.float32)

    def add_range(lo, hi):
        def body(m, carry):
            half = (m + 1) // 2
            dz = jnp.where(m % 2 == 0, half, -half)
            for k in range(3):
                from_twin(dz, m, k).wait_recv()
            add(m, 0)
            add(m, 1)
            return carry
        lax.fori_loop(lo, hi, body, 0)

    own = []
    for s in range(2):
        ref, slot = ((left, left_slot(0, True)), (right, right_slot(0, 0)))[s]
        own.append(pltpu.make_async_copy(tiles_ref, ref.at[slot, pl.ds(0, SLOTS * TILE)], own_sem.at[s]))
    for copy in own:
        copy.start()
    barrier = pltpu.get_barrier_semaphore()
    greeted = [at_z(1), at_z(-1), twin, at_xy(1, 0), at_xy(-1, 0), at_xy(0, 1), at_xy(0, -1)]
    for device in greeted:
        pl.semaphore_signal(barrier, inc=1, device_id=device, device_id_type=MESH)
    place = lax.broadcasted_iota(jnp.int32, (MARK, TILE), 0)
    marks = jnp.full((MARK, TILE), -1.0, jnp.float32)
    for s in range(SLOTS):
        code = jnp.where(s < count_ref[0, 0], rows_ref[0, 0, s] * 2 + cols_ref[0, 0, s], -1)
        marks = jnp.where(place == s, code.astype(jnp.float32), marks)
    marks = marks.astype(jnp.bfloat16)
    left[left_slot(0, True), pl.ds(SLOTS * TILE, MARK), :] = marks
    right[right_slot(0, 0), pl.ds(SLOTS * TILE, MARK), :] = marks
    out_ref[...] = jnp.zeros_like(out_ref)
    for copy in own:
        copy.wait()
    pl.semaphore_wait(barrier, len(greeted))

    for k in range(3):
        ring(1, 0, k).start()
        ring(-1, 0, k).start()
    for n in (0, 1, 4, 5):
        go(n)
    for k in range(3):
        to_twin(0, 0, k).start()

    def step_xy(d):
        if d == 1:
            come(0); go(2); go(8); go(9)
            come(1); go(3); go(12); go(13)
            come(4); go(6)
            come(5); go(7)
        elif d == 2:
            come(2); come(3); go(16); go(17)
        elif d == 3:
            come(8); go(10); come(9); go(11)
            come(12); go(14); come(13); go(15)
        elif d == 4:
            come(16); go(18); come(17); go(19)
        elif d == 5:
            for n in (6, 7, 10, 11, 14, 15, 18, 19):
                come(n)

    work = {
        (5, 0): (0, 2), (5, 1): (2, 4), (5, 2): (4, 6),
        (6, 0): (6, 8), (6, 1): (8, 10), (6, 2): (10, 11),
        (7, 0): (11, 12), (7, 1): (12, 13),
    }
    for d in range(1, 8):
        for k in range(3):
            for way in (1, -1):
                ring_in(way, d, k).wait_recv()
                if d < 7:
                    ring(way, d, k).start()
                to_twin(-way * d, 2 * d - 1 if way > 0 else 2 * d, k).start()
            if d == 7:
                far(k).start()
            if k == 0:
                step_xy(d)
            if (d, k) in work:
                add_range(*work[d, k])
    add_range(13, 15)
    for k in range(3):
        far_in(k).wait_recv()
        to_twin(8, 15, k).start()
    add_range(15, 16)

    for k in range(3):
        for d in range(7):
            for way in (1, -1):
                ring(way, d, k).wait_send()
        far(k).wait_send()
        for m in range(16):
            half = (m + 1) // 2
            to_twin(half if m % 2 == 0 else -half, m, k).wait_send()
    for n in moves:
        along(n, *moves[n]).wait_send()


def local(tile_data, block_rows, block_cols, filled_count):
    tiles = tile_data.reshape(SLOTS * TILE, TILE)
    smem = pl.BlockSpec(memory_space=pltpu.SMEM)
    return pl.pallas_call(
        kernel,
        out_shape=jax.ShapeDtypeStruct((2 * TILE, 2 * TILE), jnp.float32),
        in_specs=[smem, smem, smem, pl.BlockSpec(memory_space=pl.ANY)],
        out_specs=pl.BlockSpec(memory_space=pltpu.VMEM),
        scratch_shapes=[
            pltpu.VMEM((N_COL, ROWS, TILE), jnp.bfloat16),
            pltpu.VMEM((N_ROW, ROWS, TILE), jnp.bfloat16),
            pltpu.SemaphoreType.DMA((2,)),
            pltpu.SemaphoreType.DMA((2, 7, 3)),
            pltpu.SemaphoreType.DMA((2, 7, 3)),
            pltpu.SemaphoreType.DMA((3,)),
            pltpu.SemaphoreType.DMA((3,)),
            pltpu.SemaphoreType.DMA((16, 3)),
            pltpu.SemaphoreType.DMA((16, 3)),
            pltpu.SemaphoreType.DMA((20,)),
            pltpu.SemaphoreType.DMA((20,)),
        ],
        compiler_params=pltpu.CompilerParams(
            collective_id=0, has_side_effects=True, vmem_limit_bytes=24 * 1024 * 1024
        ),
        cost_estimate=pl.CostEstimate(
            flops=2 * 256 * 256 * 8192, bytes_accessed=1 << 20, transcendentals=0
        ),
    )(block_rows, block_cols, filled_count, tiles)


def solution(mesh):
    in_specs = (
        P("row", "col", None, None, None),
        P("row", "col", None),
        P("row", "col", None),
        P("row", "col"),
    )
    out_specs = P(("row", "layer"), "col")
    return jax.shard_map(local, mesh=mesh, in_specs=in_specs, out_specs=out_specs, check_vma=False)
```

```python
import functools

import jax
import jax.numpy as jnp
from jax import lax
from jax.experimental import pallas as pl
from jax.experimental.pallas import tpu as pltpu
from jax.sharding import PartitionSpec as P

TILE = 128
SLOTS = 3
NX, NY, NZ = 4, 8, 16
Y_LO = 4
N_ROW = 16
N_COL = 32
MARK = 16
ROWS = SLOTS * TILE + MARK
CHUNKS = ((0, 128), (128, 128), (256, 144))
PIECES = len(CHUNKS)
FIRST, SECOND, WHOLE = (0, 208), (208, 192), (0, ROWS)
MESH = pl.DeviceIdType.MESH
ONWARD = {0: (1,), 1: (1,), 2: (1,), 3: (1,), 4: (1,), 5: (1,), 6: (1,), 7: (1,)}
ORDER = (1, 2, 3, 4, 5, 6, 7)
SENT = sum(2 for d, hops in ONWARD.items() for h in hops)
REACH = sorted({h for hops in ONWARD.values() for h in hops})
WORK = {4: (0, 1), 5: (2, 3, 4), 6: (5, 6, 7), 7: (8,)}
EARLY = 6


def kernel(
    tiles_ref, rows_ref, cols_ref, count_ref, out_ref,
    left, right, rows_s, cols_s, count_s, own_sem,
    left_s, ring_r, far_r, twin_r, right_s, right_r,
):
    row = lax.axis_index("row")
    col = lax.axis_index("col")
    layer = lax.axis_index("layer")
    x, y = row // Y_LO, layer * Y_LO + row % Y_LO
    z, core = col // 2, col % 2
    other = 1 - core
    away = 1 - 2 * core
    def at_xy(axis, way):
        def make():
            on_x = other if axis == 0 else core
            nx = lax.rem(x + way * on_x + NX, NX)
            ny = lax.rem(y + way * (1 - on_x) + NY, NY)
            return (nx * Y_LO + lax.rem(ny, Y_LO), col, ny // Y_LO)

        return make()

    def right_slot(f, g):
        f, g = (2 if f == -2 else f), (2 if g == -2 else g)

        def make():
            cx = lax.rem(x + f * other + g * core + NX, NX)
            cy = lax.rem(y + f * core + g * other + NY, Y_LO)
            return cx * Y_LO + cy

        return make()

    def remote(ref, slot, span, send, recv, device):
        part = ref.at[slot, pl.ds(span[0], span[1])]
        return pltpu.make_async_remote_copy(
            src_ref=part, dst_ref=part, send_sem=send, recv_sem=recv,
            device_id=device, device_id_type=MESH,
        )

    twin = (row, z * 2 + other, layer)

    def source(dist):
        return lax.rem(z - dist * away + NZ, NZ)

    def chip_on(hops):
        return lax.rem(z + hops * away + NZ, NZ)

    def first(way, hops, k):
        chip = lax.rem(z + way * hops + NZ, NZ)
        device = (row, chip * 2 + (0 if way > 0 else 1), layer)
        return remote(left, z * 2 + core, CHUNKS[k], left_s.at[0], ring_r.at[hops - 1, core, k], device)

    def ring(dist, hops, q, k):
        slot, device = source(dist) * 2 + q, (row, chip_on(hops) * 2 + core, layer)
        return remote(left, slot, CHUNKS[k], left_s.at[0], ring_r.at[dist + hops - 1, q, k], device)

    def ring_in(dist, q, k):
        return remote(left, source(dist) * 2 + q, CHUNKS[k], left_s.at[0], ring_r.at[dist - 1, q, k], twin)

    def far(i, k, hops=0):
        slot = source(8 - hops) * 2 + (other if i and not hops else core)
        device = (row, chip_on(hops) * 2 + (other if i else core), layer)
        return remote(left, slot, CHUNKS[k], left_s.at[0], far_r.at[i, k], device)

    def to_twin(dist, q, arrived=False):
        chip = lax.rem(z + dist * away + NZ, NZ) if arrived else source(dist)
        return remote(left, chip * 2 + q, WHOLE, left_s.at[1], twin_r.at[dist, q], twin)

    def own_to_twin(arrived=False):
        return remote(left, z * 2 + (other if arrived else core), WHOLE, left_s.at[1], twin_r.at[0, 0], twin)

    moves = []
    for axis, fs in ((0, (0,)), (1, (0, -1, 1, 2))):
        for f in fs:
            moves += [(f, 0, span, axis, way) for span, way in ((WHOLE, 1), (WHOLE, -1), (FIRST, 2), (SECOND, -2))]

    def along(n, arrived=False):
        f, g, span, axis, way = moves[n]
        if arrived:
            f, g = (f - way, g) if axis == 0 else (f, g - way)
        return remote(right, right_slot(f, g), span, right_s.at[0], right_r.at[n], at_xy(axis, way))

    def go(*numbers):
        for n in numbers:
            along(n).start()

    def come(*numbers):
        for n in numbers:
            along(n, True).wait_recv()

    def picked(ref, slot, codes):
        marks = ref[slot, pl.ds(SLOTS * TILE, MARK), :].astype(jnp.float32)
        tiles = [ref[slot, pl.ds(s * TILE, TILE), :] for s in range(SLOTS)]
        blocks = []
        for code in codes:
            total = None
            for s in range(SLOTS):
                hit = jnp.where(marks[s:s + 1, :] == code, 1.0, 0.0).astype(jnp.bfloat16)
                term = tiles[s] * hit
                total = term if total is None else total + term
            blocks.append(total)
        top, low = jnp.concatenate(blocks[:2], axis=1), jnp.concatenate(blocks[2:], axis=1)
        return jnp.concatenate([top, low], axis=0)

    base = (4 * layer).astype(jnp.float32)

    def add(r):
        for q in range(2):
            lhs = picked(left, r * 2 + q, [base + i for i in range(4)])
            rhs = picked(right, r, [float(4 * q + i) for i in range(4)])
            out_ref[...] += jnp.dot(lhs, rhs, preferred_element_type=jnp.float32)

    def add_steps(*dists):
        for dist in dists:
            if dist == 0:
                own_to_twin(True).wait_recv()
            elif dist < 8:
                to_twin(dist, 0, True).wait_recv()
                to_twin(dist, 1, True).wait_recv()
            if dist in (0, 8):
                add(source(dist))
            else:
                def body(i, carry):
                    add(lax.rem(z + dist * (2 * i - 1) + NZ, NZ))
                    return carry

                lax.fori_loop(0, 2, body, 0)

    barrier = pltpu.get_barrier_semaphore()
    greeted = [twin]
    for h in REACH:
        greeted += [(row, lax.rem(z + w * h + NZ, NZ) * 2 + c, layer) for w in (1, -1) for c in (0, 1)]
    greeted += [at_xy(axis, way) for axis in (0, 1) for way in (1, -1, 2, -2)]
    for device in greeted:
        pl.semaphore_signal(barrier, inc=1, device_id=device, device_id_type=MESH)
    own = [
        pltpu.make_async_copy(rows_ref, rows_s, own_sem.at[0]),
        pltpu.make_async_copy(cols_ref, cols_s, own_sem.at[1]),
        pltpu.make_async_copy(count_ref, count_s, own_sem.at[2]),
        pltpu.make_async_copy(tiles_ref, left.at[z * 2 + core, pl.ds(0, SLOTS * TILE)], own_sem.at[3]),
        pltpu.make_async_copy(tiles_ref, right.at[right_slot(0, 0), pl.ds(0, SLOTS * TILE)], own_sem.at[4]),
    ]
    for copy in own:
        copy.start()
    for copy in own[:3]:
        copy.wait()
    place = lax.broadcasted_iota(jnp.int32, (MARK, TILE), 0)
    marks = jnp.full((MARK, TILE), -1.0, jnp.float32)
    for s in range(SLOTS):
        code = jnp.where(s < count_s[0, 0], rows_s[0, 0, s] * 2 + cols_s[0, 0, s], -1)
        marks = jnp.where(place == s, code.astype(jnp.float32), marks)
    marks = marks.astype(jnp.bfloat16)
    left[z * 2 + core, pl.ds(SLOTS * TILE, MARK), :] = marks
    right[right_slot(0, 0), pl.ds(SLOTS * TILE, MARK), :] = marks
    for copy in own[3:]:
        copy.wait()
    pl.semaphore_wait(barrier, len(greeted))

    for hops in ONWARD[0]:
        for k in range(PIECES):
            first(1, hops, k).start()
            first(-1, hops, k).start()
    go(*range(4))
    own_to_twin().start()
    out_ref[...] = jnp.zeros_like(out_ref)

    def panel(step):
        if step == 0:
            go(*range(4, 8))
        elif step == 1:
            come(0)
            go(*range(8, 12))
            come(1)
            go(*range(12, 16))
        else:
            come(2, 3)
            go(*range(16, 20))

    panel_first = jnp.logical_and(z >= 1, z < 5)

    @pl.when(panel_first)
    def _():
        for step in range(3):
            panel(step)


    for step, d in enumerate(ORDER):
        for k in range(PIECES):
            for hops in ONWARD.get(d, ()):
                for q in range(2):
                    if hops == ONWARD[d][0]:
                        ring_in(d, q, k).wait_recv()
                    if d + hops < 8:
                        ring(d, hops, q, k).start()
                if d + hops == 8:
                    far(0, k, hops).start()
                    far(1, k, hops).start()
            if d not in ONWARD:
                for q in range(2):
                    ring_in(d, q, k).wait_recv()
        to_twin(d, 0).start()
        to_twin(d, 1).start()
        if step < 3:
            pl.when(jnp.logical_not(panel_first))(functools.partial(panel, step))
        if step in WORK:

            @pl.when(z < EARLY)
            def _(step=step):
                if step == 4:
                    come(*range(4, 20))
                add_steps(*WORK[step])

    for k in range(PIECES):
        for i in range(2):
            far(i, k).wait_recv()

    @pl.when(z < EARLY)
    def _():
        add_steps(*WORK[7])

    @pl.when(z >= EARLY)
    def _():
        come(*range(4, 20))
        own_to_twin(True).wait_recv()
        for dist in range(1, 8):
            for q in range(2):
                to_twin(dist, q, True).wait_recv()

        def body(i, carry):
            add(i)
            return carry

        lax.fori_loop(0, N_ROW, body, 0)

    for i, cells in ((0, SENT), (1, 15)):
        sent = left.at[pl.ds(0, cells)]
        pltpu.make_async_copy(sent, sent, left_s.at[i]).wait()
    sent = right.at[pl.ds(0, 15)]
    pltpu.make_async_copy(sent, sent, right_s.at[0]).wait()


def local(tile_data, block_rows, block_cols, filled_count):
    tiles = tile_data.reshape(SLOTS * TILE, TILE)
    hbm = pl.BlockSpec(memory_space=pltpu.HBM)
    return pl.pallas_call(
        kernel,
        out_shape=jax.ShapeDtypeStruct((2 * TILE, 2 * TILE), jnp.float32),
        in_specs=[hbm, hbm, hbm, hbm],
        out_specs=pl.BlockSpec(memory_space=pltpu.VMEM),
        scratch_shapes=[
            pltpu.VMEM((N_COL, ROWS, TILE), jnp.bfloat16),
            pltpu.VMEM((N_ROW, ROWS, TILE), jnp.bfloat16),
            pltpu.SMEM((1, 1, SLOTS), jnp.int32),
            pltpu.SMEM((1, 1, SLOTS), jnp.int32),
            pltpu.SMEM((1, 1), jnp.int32),
            pltpu.SemaphoreType.DMA((5,)),
            pltpu.SemaphoreType.DMA((2,)),
            pltpu.SemaphoreType.DMA((7, 2, PIECES)),
            pltpu.SemaphoreType.DMA((2, PIECES)),
            pltpu.SemaphoreType.DMA((8, 2)),
            pltpu.SemaphoreType.DMA((1,)),
            pltpu.SemaphoreType.DMA((20,)),
        ],
        compiler_params=pltpu.CompilerParams(
            collective_id=0, has_side_effects=True, vmem_limit_bytes=24 * 1024 * 1024
        ),
        cost_estimate=pl.CostEstimate(
            flops=2 * 256 * 256 * 8192, bytes_accessed=1 << 20, transcendentals=0
        ),
    )(tiles, block_rows, block_cols, filled_count)


def solution(mesh):
    in_specs = (
        P("row", "col", None, None, None),
        P("row", "col", None),
        P("row", "col", None),
        P("row", "col"),
    )
    out_specs = P(("row", "layer"), "col")
    return jax.shard_map(local, mesh=mesh, in_specs=in_specs, out_specs=out_specs, check_vma=False)
```

```python
import functools

import jax
import jax.numpy as jnp
from jax import lax
from jax.experimental import pallas as pl
from jax.experimental.pallas import tpu as pltpu
from jax.sharding import PartitionSpec as P

TILE = 128
SLOTS = 3
NX, NY, NZ = 4, 8, 16
Y_LO = 4
N_ROW = 16
N_COL = 32
MARK = 16
ROWS = SLOTS * TILE + MARK
CHUNKS = ((0, 128), (128, 128), (256, 144))
PIECES = len(CHUNKS)
FIRST, SECOND, WHOLE = (0, 208), (208, 192), (0, ROWS)
MESH = pl.DeviceIdType.MESH
ONWARD = {0: (1,), 1: (1,), 2: (1,), 3: (1,), 4: (1,), 5: (1,), 6: (1,), 7: (1,)}
ORDER = (1, 2, 3, 4, 5, 6, 7)
SENT = sum(2 for d, hops in ONWARD.items() for h in hops)
EXPRESS = (8, 9)
HUB = 7
PASS_ON = 5
REACH = sorted({h for hops in ONWARD.values() for h in hops})
WORK = {5: (0, 1, 2, 3), 6: (4, 5, 6, 7), 7: (8,)}
EARLY = 6


def kernel(
    tiles_ref, rows_ref, cols_ref, count_ref, out_ref,
    left, right, rows_s, cols_s, count_s, own_sem,
    left_s, ring_r, far_r, twin_r, express_r, right_s, right_r,
):
    row = lax.axis_index("row")
    col = lax.axis_index("col")
    layer = lax.axis_index("layer")
    x, y = row // Y_LO, layer * Y_LO + row % Y_LO
    z, core = col // 2, col % 2
    other = 1 - core
    away = 1 - 2 * core
    def at_xy(axis, way):
        def make():
            on_x = other if axis == 0 else core
            nx = lax.rem(x + way * on_x + NX, NX)
            ny = lax.rem(y + way * (1 - on_x) + NY, NY)
            return (nx * Y_LO + lax.rem(ny, Y_LO), col, ny // Y_LO)

        return make()

    def right_slot(f, g):
        f, g = (2 if f == -2 else f), (2 if g == -2 else g)

        def make():
            cx = lax.rem(x + f * other + g * core + NX, NX)
            cy = lax.rem(y + f * core + g * other + NY, Y_LO)
            return cx * Y_LO + cy

        return make()

    def remote(ref, slot, span, send, recv, device):
        part = ref.at[slot, pl.ds(span[0], span[1])]
        return pltpu.make_async_remote_copy(
            src_ref=part, dst_ref=part, send_sem=send, recv_sem=recv,
            device_id=device, device_id_type=MESH,
        )

    twin = (row, z * 2 + other, layer)

    def source(dist):
        return lax.rem(z - dist * away + NZ, NZ)

    def chip_on(hops):
        return lax.rem(z + hops * away + NZ, NZ)

    def first(way, hops, k):
        chip = lax.rem(z + way * hops + NZ, NZ)
        device = (row, chip * 2 + (0 if way > 0 else 1), layer)
        return remote(left, z * 2 + core, CHUNKS[k], left_s.at[0], ring_r.at[hops - 1, core, k], device)

    def ring(dist, hops, q, k):
        slot, device = source(dist) * 2 + q, (row, chip_on(hops) * 2 + core, layer)
        return remote(left, slot, CHUNKS[k], left_s.at[0], ring_r.at[dist + hops - 1, q, k], device)

    def ring_in(dist, q, k):
        return remote(left, source(dist) * 2 + q, CHUNKS[k], left_s.at[0], ring_r.at[dist - 1, q, k], twin)

    def far(i, k, hops=0):
        slot = source(8 - hops) * 2 + (other if i and not hops else core)
        device = (row, chip_on(hops) * 2 + (other if i else core), layer)
        return remote(left, slot, CHUNKS[k], left_s.at[0], far_r.at[i, k], device)

    def to_twin(dist, q, arrived=False):
        chip = lax.rem(z + dist * away + NZ, NZ) if arrived else source(dist)
        return remote(left, chip * 2 + q, WHOLE, left_s.at[1], twin_r.at[dist, q], twin)

    zero_up = jnp.logical_and(z == 0, core == 0)
    zero_down = jnp.logical_and(z == 0, core == 1)
    before_zero = jnp.logical_and(z == NZ - 1, core == 0)
    after_zero = jnp.logical_and(z == 1, core == 1)

    def express(i, q):
        return remote(left, EXPRESS[i] * 2 + q, WHOLE, left_s.at[2], express_r.at[i, q], (row, 1, layer))

    def express_on(i, q):
        return remote(left, EXPRESS[i] * 2 + q, WHOLE, left_s.at[1], express_r.at[i, q], (row, 0, layer))

    hub = jnp.logical_and(z == HUB, core == 1)
    parcels = [(i, q) for i in range(len(EXPRESS)) for q in range(2)]

    def own_to_twin(arrived=False):
        return remote(left, z * 2 + (other if arrived else core), WHOLE, left_s.at[1], twin_r.at[0, 0], twin)

    moves = []
    for axis, fs in ((0, (0,)), (1, (0, -1, 1, 2))):
        for f in fs:
            moves += [(f, 0, span, axis, way) for span, way in ((WHOLE, 1), (WHOLE, -1), (FIRST, 2), (SECOND, -2))]

    def along(n, arrived=False):
        f, g, span, axis, way = moves[n]
        if arrived:
            f, g = (f - way, g) if axis == 0 else (f, g - way)
        return remote(right, right_slot(f, g), span, right_s.at[0], right_r.at[n], at_xy(axis, way))

    def go(*numbers):
        for n in numbers:
            along(n).start()

    def come(*numbers):
        for n in numbers:
            along(n, True).wait_recv()

    def picked(ref, slot, codes):
        marks = ref[slot, pl.ds(SLOTS * TILE, MARK), :]
        wide = [jnp.broadcast_to(marks[s:s + 1, :], (TILE, TILE)) for s in range(SLOTS)]
        tiles = [ref[slot, pl.ds(s * TILE, TILE), :] for s in range(SLOTS)]
        blocks = []
        for code in codes:
            total = jnp.zeros((TILE, TILE), jnp.bfloat16)
            for s in range(SLOTS):
                total = jnp.where(wide[s] == jnp.asarray(code, jnp.bfloat16), tiles[s], total)
            blocks.append(total)
        top, low = jnp.concatenate(blocks[:2], axis=1), jnp.concatenate(blocks[2:], axis=1)
        return jnp.concatenate([top, low], axis=0)

    base = (4 * layer).astype(jnp.float32)

    def add(r):
        for q in range(2):
            lhs = picked(left, r * 2 + q, [base + i for i in range(4)])
            rhs = picked(right, r, [float(4 * q + i) for i in range(4)])
            out_ref[...] += jnp.dot(lhs, rhs, preferred_element_type=jnp.float32)

    def add_steps(*dists):
        for dist in dists:
            if dist == 0:
                own_to_twin(True).wait_recv()
            elif dist < 8:
                def other_way(dist=dist):
                    to_twin(dist, 0, True).wait_recv()
                    to_twin(dist, 1, True).wait_recv()

                if dist == 7:
                    pl.when(jnp.logical_not(zero_down))(other_way)
                else:
                    other_way()
            if dist in (0, 8):
                add(source(dist))
            else:
                def body(i, carry):
                    add(lax.rem(z + dist * (2 * i - 1) + NZ, NZ))
                    return carry

                lax.fori_loop(0, 2, body, 0)

    barrier = pltpu.get_barrier_semaphore()
    greeted = [twin]
    for h in REACH:
        greeted += [(row, lax.rem(z + w * h + NZ, NZ) * 2 + c, layer) for w in (1, -1) for c in (0, 1)]
    greeted += [at_xy(axis, way) for axis in (0, 1) for way in (1, -1, 2, -2)]
    for device in greeted:
        pl.semaphore_signal(barrier, inc=1, device_id=device, device_id_type=MESH)
    @pl.when(zero_down)
    def _():
        peer = (row, HUB * 2 + 1, layer)
        pl.semaphore_signal(barrier, inc=1, device_id=peer, device_id_type=MESH)

    own = [
        pltpu.make_async_copy(rows_ref, rows_s, own_sem.at[0]),
        pltpu.make_async_copy(cols_ref, cols_s, own_sem.at[1]),
        pltpu.make_async_copy(count_ref, count_s, own_sem.at[2]),
        pltpu.make_async_copy(tiles_ref, left.at[z * 2 + core, pl.ds(0, SLOTS * TILE)], own_sem.at[3]),
        pltpu.make_async_copy(tiles_ref, right.at[right_slot(0, 0), pl.ds(0, SLOTS * TILE)], own_sem.at[4]),
    ]
    for copy in own:
        copy.start()
    for copy in own[:3]:
        copy.wait()
    place = lax.broadcasted_iota(jnp.int32, (MARK, TILE), 0)
    marks = jnp.full((MARK, TILE), -1.0, jnp.float32)
    for s in range(SLOTS):
        code = jnp.where(s < count_s[0, 0], rows_s[0, 0, s] * 2 + cols_s[0, 0, s], -1)
        marks = jnp.where(place == s, code.astype(jnp.float32), marks)
    marks = marks.astype(jnp.bfloat16)
    left[z * 2 + core, pl.ds(SLOTS * TILE, MARK), :] = marks
    right[right_slot(0, 0), pl.ds(SLOTS * TILE, MARK), :] = marks
    for copy in own[3:]:
        copy.wait()
    pl.semaphore_wait(barrier, len(greeted) + jnp.where(hub, 1, 0))

    for hops in ONWARD[0]:
        for k in range(PIECES):
            first(1, hops, k).start()
            first(-1, hops, k).start()
    go(*range(4))
    own_to_twin().start()
    out_ref[...] = jnp.zeros_like(out_ref)

    def panel(step):
        if step == 0:
            go(*range(4, 8))
        elif step == 1:
            come(0)
            go(*range(8, 12))
            come(1)
            go(*range(12, 16))
        else:
            come(2, 3)
            go(*range(16, 20))

    panel_first = jnp.logical_and(z >= 1, z < 5)

    @pl.when(panel_first)
    def _():
        for step in range(3):
            panel(step)


    def last_ring():
        for k in range(PIECES):
            for q in range(2):
                ring_in(7, q, k).wait_recv()

            @pl.when(jnp.logical_not(jnp.logical_or(before_zero, after_zero)))
            def _(k=k):
                far(0, k, 1).start()
                far(1, k, 1).start()

        to_twin(7, 0).start()
        to_twin(7, 1).start()

    def last_zero():
        for i, q in parcels:
            express_on(i, q).wait_recv()
        for k in range(PIECES):
            far(0, k, 1).start()
            far(1, k, 1).start()

    for step, d in enumerate(ORDER):
        if d == 7:
            pl.when(jnp.logical_not(zero_up))(last_ring)
            pl.when(zero_up)(last_zero)
        else:
            for k in range(PIECES):
                for q in range(2):
                    ring_in(d, q, k).wait_recv()
                    if d == 6:
                        pl.when(jnp.logical_not(before_zero))(ring(d, 1, q, k).start)
                    else:
                        ring(d, 1, q, k).start()
            to_twin(d, 0).start()
            to_twin(d, 1).start()
        if 1 <= d <= len(EXPRESS):

            @pl.when(hub)
            def _(i=d - 1):
                for q in range(2):
                    express(i, q).start()

        if d == PASS_ON:

            @pl.when(zero_down)
            def _():
                for i, q in parcels:
                    express(i, q).wait_recv()
                    express_on(i, q).start()

        if step < 3:
            pl.when(jnp.logical_not(panel_first))(functools.partial(panel, step))
        if step in WORK:

            @pl.when(z < EARLY)
            def _(step=step):
                if step == 5:
                    come(*range(4, 20))
                add_steps(*WORK[step])

    @pl.when(z != 0)
    def _():
        for k in range(PIECES):
            for i in range(2):
                far(i, k).wait_recv()

    @pl.when(z < EARLY)
    def _():
        add_steps(*WORK[7])

    @pl.when(z >= EARLY)
    def _():
        come(*range(4, 20))
        own_to_twin(True).wait_recv()
        for dist in range(1, 8):
            for q in range(2):
                to_twin(dist, q, True).wait_recv()

        def body(i, carry):
            add(i)
            return carry

        lax.fori_loop(0, N_ROW, body, 0)

    def left_by(i, cells):
        sent = left.at[pl.ds(0, cells)]
        pltpu.make_async_copy(sent, sent, left_s.at[i]).wait()

    usual = jnp.logical_not(jnp.logical_or(before_zero, after_zero))
    pl.when(usual)(lambda: left_by(0, SENT))
    pl.when(before_zero)(lambda: left_by(0, SENT - 4))
    pl.when(after_zero)(lambda: left_by(0, SENT - 2))
    pl.when(z != 0)(lambda: left_by(1, 15))
    pl.when(zero_down)(lambda: left_by(1, 15 + len(parcels)))
    pl.when(zero_up)(lambda: left_by(1, 13))
    pl.when(hub)(lambda: left_by(2, len(parcels)))
    sent = right.at[pl.ds(0, 15)]
    pltpu.make_async_copy(sent, sent, right_s.at[0]).wait()


def local(tile_data, block_rows, block_cols, filled_count):
    tiles = tile_data.reshape(SLOTS * TILE, TILE)
    hbm = pl.BlockSpec(memory_space=pltpu.HBM)
    return pl.pallas_call(
        kernel,
        out_shape=jax.ShapeDtypeStruct((2 * TILE, 2 * TILE), jnp.float32),
        in_specs=[hbm, hbm, hbm, hbm],
        out_specs=pl.BlockSpec(memory_space=pltpu.VMEM),
        scratch_shapes=[
            pltpu.VMEM((N_COL, ROWS, TILE), jnp.bfloat16),
            pltpu.VMEM((N_ROW, ROWS, TILE), jnp.bfloat16),
            pltpu.SMEM((1, 1, SLOTS), jnp.int32),
            pltpu.SMEM((1, 1, SLOTS), jnp.int32),
            pltpu.SMEM((1, 1), jnp.int32),
            pltpu.SemaphoreType.DMA((5,)),
            pltpu.SemaphoreType.DMA((3,)),
            pltpu.SemaphoreType.DMA((7, 2, PIECES)),
            pltpu.SemaphoreType.DMA((2, PIECES)),
            pltpu.SemaphoreType.DMA((8, 2)),
            pltpu.SemaphoreType.DMA((len(EXPRESS), 2)),
            pltpu.SemaphoreType.DMA((1,)),
            pltpu.SemaphoreType.DMA((20,)),
        ],
        compiler_params=pltpu.CompilerParams(
            collective_id=0, has_side_effects=True, vmem_limit_bytes=24 * 1024 * 1024
        ),
        cost_estimate=pl.CostEstimate(
            flops=2 * 256 * 256 * 8192, bytes_accessed=1 << 20, transcendentals=0
        ),
    )(tiles, block_rows, block_cols, filled_count)


def solution(mesh):
    in_specs = (
        P("row", "col", None, None, None),
        P("row", "col", None),
        P("row", "col", None),
        P("row", "col"),
    )
    out_specs = P(("row", "layer"), "col")
    return jax.shard_map(local, mesh=mesh, in_specs=in_specs, out_specs=out_specs, check_vma=False)
```

```python
import functools

import jax
import jax.numpy as jnp
from jax import lax
from jax.experimental import pallas as pl
from jax.experimental.pallas import tpu as pltpu
from jax.sharding import PartitionSpec as P

TILE = 128
SLOTS = 3
NX, NY, NZ = 4, 8, 16
Y_LO = 4
N_ROW = 16
N_COL = 32
MARK = 16
ROWS = SLOTS * TILE + MARK
CHUNKS = ((0, 128), (128, 128), (256, 144))
PIECES = len(CHUNKS)
FIRST, SECOND, WHOLE = (0, 208), (208, 192), (0, ROWS)
MESH = pl.DeviceIdType.MESH
ONWARD = {0: (1,), 1: (1,), 2: (1,), 3: (1,), 4: (1,), 5: (1,), 6: (1,), 7: (1,)}
ORDER = (1, 2, 3, 4, 5, 6, 7)
SENT = sum(2 for d, hops in ONWARD.items() for h in hops)
EXPRESS = (8, 9)
HUB = 7
PASS_ON = 5
REACH = sorted({h for hops in ONWARD.values() for h in hops})
WORK = {5: (0, 1, 2), 6: (3, 4, 5, 6, 7), 7: (8,)}
EARLY = 6


def kernel(
    tiles_ref, rows_ref, cols_ref, count_ref, out_ref,
    left, right, rows_s, cols_s, count_s, own_sem,
    left_s, ring_r, far_r, twin_r, express_r, right_s, right_r,
):
    row = lax.axis_index("row")
    col = lax.axis_index("col")
    layer = lax.axis_index("layer")
    x, y = row // Y_LO, layer * Y_LO + row % Y_LO
    z, core = col // 2, col % 2
    other = 1 - core
    away = 1 - 2 * core
    def at_xy(axis, way):
        def make():
            on_x = other if axis == 0 else core
            nx = lax.rem(x + way * on_x + NX, NX)
            ny = lax.rem(y + way * (1 - on_x) + NY, NY)
            return (nx * Y_LO + lax.rem(ny, Y_LO), col, ny // Y_LO)

        return make()

    def right_slot(f, g):
        f, g = (2 if f == -2 else f), (2 if g == -2 else g)

        def make():
            cx = lax.rem(x + f * other + g * core + NX, NX)
            cy = lax.rem(y + f * core + g * other + NY, Y_LO)
            return cx * Y_LO + cy

        return make()

    def remote(ref, slot, span, send, recv, device):
        part = ref.at[slot, pl.ds(span[0], span[1])]
        return pltpu.make_async_remote_copy(
            src_ref=part, dst_ref=part, send_sem=send, recv_sem=recv,
            device_id=device, device_id_type=MESH,
        )

    twin = (row, z * 2 + other, layer)

    def source(dist):
        return lax.rem(z - dist * away + NZ, NZ)

    def chip_on(hops):
        return lax.rem(z + hops * away + NZ, NZ)

    def first(way, hops, k):
        chip = lax.rem(z + way * hops + NZ, NZ)
        device = (row, chip * 2 + (0 if way > 0 else 1), layer)
        return remote(left, z * 2 + core, CHUNKS[k], left_s.at[0], ring_r.at[hops - 1, core, k], device)

    def ring(dist, hops, q, k):
        slot, device = source(dist) * 2 + q, (row, chip_on(hops) * 2 + core, layer)
        return remote(left, slot, CHUNKS[k], left_s.at[0], ring_r.at[dist + hops - 1, q, k], device)

    def ring_in(dist, q, k):
        return remote(left, source(dist) * 2 + q, CHUNKS[k], left_s.at[0], ring_r.at[dist - 1, q, k], twin)

    def far(i, k, hops=0):
        slot = source(8 - hops) * 2 + (other if i and not hops else core)
        device = (row, chip_on(hops) * 2 + (other if i else core), layer)
        return remote(left, slot, CHUNKS[k], left_s.at[0], far_r.at[i, k], device)

    def to_twin(dist, q, arrived=False):
        chip = lax.rem(z + dist * away + NZ, NZ) if arrived else source(dist)
        return remote(left, chip * 2 + q, WHOLE, left_s.at[1], twin_r.at[dist, q], twin)

    zero_up = jnp.logical_and(z == 0, core == 0)
    zero_down = jnp.logical_and(z == 0, core == 1)
    before_zero = jnp.logical_and(z == NZ - 1, core == 0)
    after_zero = jnp.logical_and(z == 1, core == 1)

    def express(i, q):
        return remote(left, EXPRESS[i] * 2 + q, WHOLE, left_s.at[2], express_r.at[i, q], (row, 1, layer))

    def express_on(i, q):
        return remote(left, EXPRESS[i] * 2 + q, WHOLE, left_s.at[1], express_r.at[i, q], (row, 0, layer))

    hub = jnp.logical_and(z == HUB, core == 1)
    parcels = [(i, q) for i in range(len(EXPRESS)) for q in range(2)]

    def own_to_twin(arrived=False):
        return remote(left, z * 2 + (other if arrived else core), WHOLE, left_s.at[1], twin_r.at[0, 0], twin)

    moves = []
    for axis, fs in ((0, (0,)), (1, (0, -1, 1, 2))):
        for f in fs:
            moves += [(f, 0, span, axis, way) for span, way in ((WHOLE, 1), (WHOLE, -1), (FIRST, 2), (SECOND, -2))]

    def along(n, arrived=False):
        f, g, span, axis, way = moves[n]
        if arrived:
            f, g = (f - way, g) if axis == 0 else (f, g - way)
        return remote(right, right_slot(f, g), span, right_s.at[0], right_r.at[n], at_xy(axis, way))

    def go(*numbers):
        for n in numbers:
            along(n).start()

    def come(*numbers):
        for n in numbers:
            along(n, True).wait_recv()

    def picked(ref, slot, codes):
        marks = ref[slot, pl.ds(SLOTS * TILE, MARK), :]
        wide = [jnp.broadcast_to(marks[s:s + 1, :], (TILE, TILE)) for s in range(SLOTS)]
        tiles = [ref[slot, pl.ds(s * TILE, TILE), :] for s in range(SLOTS)]
        blocks = []
        for code in codes:
            total = jnp.zeros((TILE, TILE), jnp.bfloat16)
            for s in range(SLOTS):
                total = jnp.where(wide[s] == jnp.asarray(code, jnp.bfloat16), tiles[s], total)
            blocks.append(total)
        top, low = jnp.concatenate(blocks[:2], axis=1), jnp.concatenate(blocks[2:], axis=1)
        return jnp.concatenate([top, low], axis=0)

    base = (4 * layer).astype(jnp.float32)

    def add(r):
        for q in range(2):
            lhs = picked(left, r * 2 + q, [base + i for i in range(4)])
            rhs = picked(right, r, [float(4 * q + i) for i in range(4)])
            out_ref[...] += jnp.dot(lhs, rhs, preferred_element_type=jnp.float32)

    def add_steps(*dists):
        for dist in dists:
            if dist == 0:
                own_to_twin(True).wait_recv()
            elif dist < 8:
                def other_way(dist=dist):
                    to_twin(dist, 0, True).wait_recv()
                    to_twin(dist, 1, True).wait_recv()

                if dist == 7:
                    pl.when(jnp.logical_not(zero_down))(other_way)
                else:
                    other_way()
            if dist in (0, 8):
                add(source(dist))
            else:
                def body(i, carry):
                    add(lax.rem(z + dist * (2 * i - 1) + NZ, NZ))
                    return carry

                lax.fori_loop(0, 2, body, 0)

    barrier = pltpu.get_barrier_semaphore()
    greeted = [twin]
    for h in REACH:
        greeted += [(row, lax.rem(z + w * h + NZ, NZ) * 2 + c, layer) for w in (1, -1) for c in (0, 1)]
    greeted += [at_xy(axis, way) for axis in (0, 1) for way in (1, -1, 2, -2)]
    for device in greeted:
        pl.semaphore_signal(barrier, inc=1, device_id=device, device_id_type=MESH)
    @pl.when(zero_down)
    def _():
        peer = (row, HUB * 2 + 1, layer)
        pl.semaphore_signal(barrier, inc=1, device_id=peer, device_id_type=MESH)

    own = [
        pltpu.make_async_copy(rows_ref, rows_s, own_sem.at[0]),
        pltpu.make_async_copy(cols_ref, cols_s, own_sem.at[1]),
        pltpu.make_async_copy(count_ref, count_s, own_sem.at[2]),
        pltpu.make_async_copy(tiles_ref, left.at[z * 2 + core, pl.ds(0, SLOTS * TILE)], own_sem.at[3]),
        pltpu.make_async_copy(tiles_ref, right.at[right_slot(0, 0), pl.ds(0, SLOTS * TILE)], own_sem.at[4]),
    ]
    for copy in own:
        copy.start()
    for copy in own[:3]:
        copy.wait()
    place = lax.broadcasted_iota(jnp.int32, (MARK, TILE), 0)
    marks = jnp.full((MARK, TILE), -1.0, jnp.float32)
    for s in range(SLOTS):
        code = jnp.where(s < count_s[0, 0], rows_s[0, 0, s] * 2 + cols_s[0, 0, s], -1)
        marks = jnp.where(place == s, code.astype(jnp.float32), marks)
    marks = marks.astype(jnp.bfloat16)
    left[z * 2 + core, pl.ds(SLOTS * TILE, MARK), :] = marks
    right[right_slot(0, 0), pl.ds(SLOTS * TILE, MARK), :] = marks
    for copy in own[3:]:
        copy.wait()
    pl.semaphore_wait(barrier, len(greeted) + jnp.where(hub, 1, 0))

    for hops in ONWARD[0]:
        for k in range(PIECES):
            first(1, hops, k).start()
            first(-1, hops, k).start()
    go(*range(4))
    own_to_twin().start()
    out_ref[...] = jnp.zeros_like(out_ref)

    def panel(step):
        if step == 0:
            go(*range(4, 8))
        elif step == 1:
            come(0)
            go(*range(8, 12))
            come(1)
            go(*range(12, 16))
        else:
            come(2, 3)
            go(*range(16, 20))

    panel_first = jnp.logical_and(z >= 1, z < 5)

    @pl.when(panel_first)
    def _():
        for step in range(3):
            panel(step)


    def last_ring():
        for k in range(PIECES):
            for q in range(2):
                ring_in(7, q, k).wait_recv()

            @pl.when(jnp.logical_not(jnp.logical_or(before_zero, after_zero)))
            def _(k=k):
                far(0, k, 1).start()
                far(1, k, 1).start()

        to_twin(7, 0).start()
        to_twin(7, 1).start()

    def last_zero():
        for i, q in parcels:
            express_on(i, q).wait_recv()
        for k in range(PIECES):
            far(0, k, 1).start()
            far(1, k, 1).start()

    for step, d in enumerate(ORDER):
        if d == 7:
            pl.when(jnp.logical_not(zero_up))(last_ring)
            pl.when(zero_up)(last_zero)
        else:
            for k in range(PIECES):
                for q in range(2):
                    ring_in(d, q, k).wait_recv()
                    if d == 6:
                        pl.when(jnp.logical_not(before_zero))(ring(d, 1, q, k).start)
                    else:
                        ring(d, 1, q, k).start()
            to_twin(d, 0).start()
            to_twin(d, 1).start()
        if 1 <= d <= len(EXPRESS):

            @pl.when(hub)
            def _(i=d - 1):
                for q in range(2):
                    express(i, q).start()

        if d == PASS_ON:

            @pl.when(zero_down)
            def _():
                for i, q in parcels:
                    express(i, q).wait_recv()
                    express_on(i, q).start()

        if step < 3:
            pl.when(jnp.logical_not(panel_first))(functools.partial(panel, step))
        if step in WORK:

            @pl.when(z < EARLY)
            def _(step=step):
                if step == 5:
                    come(*range(4, 20))
                add_steps(*WORK[step])

    @pl.when(z != 0)
    def _():
        for k in range(PIECES):
            for i in range(2):
                far(i, k).wait_recv()

    @pl.when(z < EARLY)
    def _():
        add_steps(*WORK[7])

    @pl.when(z >= EARLY)
    def _():
        come(*range(4, 20))
        own_to_twin(True).wait_recv()
        for dist in range(1, 8):
            for q in range(2):
                to_twin(dist, q, True).wait_recv()

        def body(i, carry):
            add(i)
            return carry

        lax.fori_loop(0, N_ROW, body, 0)

    def left_by(i, cells):
        sent = left.at[pl.ds(0, cells)]
        pltpu.make_async_copy(sent, sent, left_s.at[i]).wait()

    usual = jnp.logical_not(jnp.logical_or(before_zero, after_zero))
    pl.when(usual)(lambda: left_by(0, SENT))
    pl.when(before_zero)(lambda: left_by(0, SENT - 4))
    pl.when(after_zero)(lambda: left_by(0, SENT - 2))
    pl.when(z != 0)(lambda: left_by(1, 15))
    pl.when(zero_down)(lambda: left_by(1, 15 + len(parcels)))
    pl.when(zero_up)(lambda: left_by(1, 13))
    pl.when(hub)(lambda: left_by(2, len(parcels)))
    sent = right.at[pl.ds(0, 15)]
    pltpu.make_async_copy(sent, sent, right_s.at[0]).wait()


def local(tile_data, block_rows, block_cols, filled_count):
    tiles = tile_data.reshape(SLOTS * TILE, TILE)
    hbm = pl.BlockSpec(memory_space=pltpu.HBM)
    return pl.pallas_call(
        kernel,
        out_shape=jax.ShapeDtypeStruct((2 * TILE, 2 * TILE), jnp.float32),
        in_specs=[hbm, hbm, hbm, hbm],
        out_specs=pl.BlockSpec(memory_space=pltpu.VMEM),
        scratch_shapes=[
            pltpu.VMEM((N_COL, ROWS, TILE), jnp.bfloat16),
            pltpu.VMEM((N_ROW, ROWS, TILE), jnp.bfloat16),
            pltpu.SMEM((1, 1, SLOTS), jnp.int32),
            pltpu.SMEM((1, 1, SLOTS), jnp.int32),
            pltpu.SMEM((1, 1), jnp.int32),
            pltpu.SemaphoreType.DMA((5,)),
            pltpu.SemaphoreType.DMA((3,)),
            pltpu.SemaphoreType.DMA((7, 2, PIECES)),
            pltpu.SemaphoreType.DMA((2, PIECES)),
            pltpu.SemaphoreType.DMA((8, 2)),
            pltpu.SemaphoreType.DMA((len(EXPRESS), 2)),
            pltpu.SemaphoreType.DMA((1,)),
            pltpu.SemaphoreType.DMA((20,)),
        ],
        compiler_params=pltpu.CompilerParams(
            collective_id=0, has_side_effects=True, vmem_limit_bytes=24 * 1024 * 1024
        ),
        cost_estimate=pl.CostEstimate(
            flops=2 * 256 * 256 * 8192, bytes_accessed=1 << 20, transcendentals=0
        ),
    )(tiles, block_rows, block_cols, filled_count)


def solution(mesh):
    in_specs = (
        P("row", "col", None, None, None),
        P("row", "col", None),
        P("row", "col", None),
        P("row", "col"),
    )
    out_specs = P(("row", "layer"), "col")
    return jax.shard_map(local, mesh=mesh, in_specs=in_specs, out_specs=out_specs, check_vma=False)
```
